256 devices in a mesh: obs: 16 (over z, x_hi), cells: 16 (over y, x_lo, core).
Axes of the slice: x: 4 (x_hi: 2, x_lo: 2; x = x_hi * 2 + x_lo), y: 4, z: 8, core: 2. Of those that a mesh axis runs over, the one named last changes fastest.
Arguments:
- adjoint_start: float32 [4096, 16, 8, 128], P('obs', 'cells'), may hold values from -8 to 8
- forward_heads: float32 [64, 16, 8, 128], P(None, 'cells'), may hold values from -6 to 6
- zone_label: int32 [16, 8, 128], P('cells'), may hold values from 0 to 15
- zone_logk: float32 [16], replicated, may hold values from -1.2 to 1.2
- obs_cell: int32 [4096], P('obs'), may hold values from 0 to 16383
- test_of_obs: int32 [4096], P('obs'), may hold values from 0 to 63
Outputs:
- sensitivity: float32 [4096, 16, 8, 128], P('obs', 'cells')
- gram: float32 [4096, 4096], P('obs', 'cells')
The draws below stay inside these ranges and needn't reach their ends.
All inputs are finite; a program needn't handle non-finite values.
Results may differ from the reference program's by a relative error of at most 0.0003.
Values sent between devices are 32-bit elements; how exact they have to be, the bound alone decides.
No kernel may reach another device: no remote copies, remote signals or barrier semaphores. Data moves between devices by JAX's collectives and lax.ppermute only.
A program may use at most 64 MiB of HBM per device.

```python
import jax
import jax.numpy as jnp
from jax import lax

NY = 8
NZ = 128
TESTS = 64
ZONES = 16
SWEEPS = 3
OBS_DEV = 256
OBS = 4096
NX = 16
NCELL = 16384
N_OBS = 16


def draw_adjoint_start(key, part):
    shape = (OBS, NX, NY, NZ)
    common = jax.random.normal(jax.random.fold_in(key, 11), (1, NX, NY, NZ), jnp.float32)
    noise = jax.random.normal(jax.random.fold_in(key, 12), shape, jnp.float32)
    values = common + 0.8 * noise
    return jnp.clip(values, -8.0, 8.0).astype(jnp.float32)


def plant(drawn, own_key, smallest, largest):
    place = [jax.random.randint(jax.random.fold_in(own_key, axis), (), 0, length) for axis, length in enumerate(drawn.shape)]
    main_axis = drawn.shape.index(max(drawn.shape))
    neighbour = place[:main_axis] + [(place[main_axis] + 1) % drawn.shape[main_axis]] + place[main_axis + 1:]
    return drawn.at[tuple(place)].set(smallest).at[tuple(neighbour)].set(largest)


def block_levels(key, dims, pieces, low, high):
    level = 1.0
    for axis_at, parts in pieces:
        steps = jax.random.uniform(jax.random.fold_in(jax.random.fold_in(key, 6), axis_at), (parts,), jnp.float32, low / len(pieces), high / len(pieces))
        level = level * jnp.repeat(jnp.exp(steps), dims[axis_at] // parts).reshape((-1,) + (1,) * (len(dims) - 1 - axis_at))
    return level


def gaussian(key, dims, spread, reach, shards=(), held_as=jnp.bfloat16):
    loudness = block_levels(key, dims, shards, -0.22, 0.18) if shards else 1.0
    values = jax.random.normal(key, dims, jnp.float32) * spread * loudness
    return jnp.minimum(jnp.maximum(values, -reach), reach).astype(held_as)


def setup_inputs(seed: int = 0) -> dict:
    key_list = jax.random.split(jax.random.key(seed), 7)
    adjoint_start = draw_adjoint_start(jax.random.fold_in(key_list[6], 71), 0)
    forward_heads = gaussian(key_list[1], (TESTS, NX, NY, NZ), 1.0, 6.0, ((1, 16),), jnp.float32)
    zone_label = plant(jax.random.randint(key_list[2], (NX, NY, NZ), 0, ZONES), jax.random.fold_in(key_list[2], 1), 0, ZONES - 1).astype(jnp.int32)
    zone_logk = jnp.clip(jax.random.uniform(key_list[3], (ZONES,), jnp.float32, -1.2, 1.2), -1.2, 1.2)
    obs_cell = plant(jax.random.randint(key_list[4], (OBS,), 0, NCELL), jax.random.fold_in(key_list[4], 1), 0, NCELL - 1).astype(jnp.int32)
    test_of_obs = plant(jax.random.randint(key_list[5], (OBS,), 0, TESTS), jax.random.fold_in(key_list[5], 1), 0, TESTS - 1).astype(jnp.int32)
    return {"adjoint_start": adjoint_start, "forward_heads": forward_heads, "zone_label": zone_label, "zone_logk": zone_logk, "obs_cell": obs_cell, "test_of_obs": test_of_obs}


source_weight = 16.0
spectrum_centre = 1.075
spectrum_halfwidth = 0.925


def conductivity(zone_label, zone_logk):
    table = jnp.exp(zone_logk)
    labels = jnp.arange(table.shape[0], dtype=jnp.int32)
    match = zone_label[None] == labels[:, None, None, None]
    return jnp.sum(jnp.where(match, table[:, None, None, None], jnp.float32(0.0)), axis=0)


def face(centre, beside):
    return jnp.where(beside > 0, 2.0 * centre * beside / (centre + beside), centre)


def neighbours(padded):
    return [padded[..., :-2, 1:-1, 1:-1], padded[..., 2:, 1:-1, 1:-1],
            padded[..., 1:-1, :-2, 1:-1], padded[..., 1:-1, 2:, 1:-1],
            padded[..., 1:-1, 1:-1, :-2], padded[..., 1:-1, 1:-1, 2:]]


def face_weights(cond_padded):
    centre = cond_padded[1:-1, 1:-1, 1:-1]
    weights = [face(centre, beside) for beside in neighbours(cond_padded)]
    diagonal = weights[0]
    for extra in weights[1:]:
        diagonal = diagonal + extra
    return weights, diagonal


def operate(padded, field, weights, diagonal):
    result = diagonal * field
    for weight, beside in zip(weights, neighbours(padded)):
        result = result - weight * beside
    return result


def gradients(padded):
    return [(padded[..., 2:, 1:-1, 1:-1] - padded[..., :-2, 1:-1, 1:-1]) * 0.5,
            (padded[..., 1:-1, 2:, 1:-1] - padded[..., 1:-1, :-2, 1:-1]) * 0.5,
            (padded[..., 1:-1, 1:-1, 2:] - padded[..., 1:-1, 1:-1, :-2]) * 0.5]


def chebyshev(start, sources, weights, diagonal, pad_field):
    ratio = spectrum_centre / spectrum_halfwidth
    adjoint = start
    update = None
    damping = 1.0 / ratio
    for sweep in range(SWEEPS):
        misfit = sources - operate(pad_field(adjoint), adjoint, weights, diagonal)
        if sweep == 0:
            update = misfit / (spectrum_centre * diagonal)
            damping = 1.0 / ratio
        else:
            newer = 1.0 / (2.0 * ratio - damping)
            update = (newer * damping) * update + (2.0 * newer / spectrum_halfwidth) * (misfit / diagonal)
            damping = newer
        adjoint = adjoint + update
    return adjoint


def sensitivity_of(adjoint_padded, head_grads, chosen, conduct):
    adjoint_grads = gradients(adjoint_padded)
    total = adjoint_grads[0] * jnp.take(head_grads[0], chosen, axis=0)
    total = total + adjoint_grads[1] * jnp.take(head_grads[1], chosen, axis=0)
    total = total + adjoint_grads[2] * jnp.take(head_grads[2], chosen, axis=0)
    return -conduct * total


def pad_spatial(field):
    return jnp.pad(field, ((0, 0), (1, 1), (1, 1), (1, 1)))


def reference(adjoint_start, forward_heads, zone_label, zone_logk, obs_cell, test_of_obs):
    conduct = conductivity(zone_label, zone_logk)
    weights, diagonal = face_weights(jnp.pad(conduct, 1))
    head_grads = gradients(pad_spatial(forward_heads))
    cell_ids = jnp.arange(NCELL, dtype=jnp.int32).reshape(NX, NY, NZ)

    def one_group(items):
        start, cells_here, tests_here = items
        sources = jnp.where(cell_ids[None] == cells_here[:, None, None, None], jnp.float32(source_weight), jnp.float32(0.0))
        adjoint = chebyshev(start, sources, weights, diagonal, pad_spatial)
        return sensitivity_of(pad_spatial(adjoint), head_grads, tests_here, conduct)

    groups = (adjoint_start.reshape(N_OBS, OBS_DEV, NX, NY, NZ),
              obs_cell.reshape(N_OBS, OBS_DEV).astype(jnp.int32),
              test_of_obs.reshape(N_OBS, OBS_DEV).astype(jnp.int32))
    sensitivity = lax.map(one_group, groups).reshape(OBS, NX, NY, NZ)
    flat = sensitivity.reshape(OBS, NCELL)
    gram = jnp.dot(flat, flat.T, preferred_element_type=jnp.float32, precision=lax.Precision.HIGHEST) * (1.0 / NCELL)
    return sensitivity, gram
```

```python
import jax
import jax.numpy as jnp
from jax import lax
from jax.experimental import pallas as pl
from jax.experimental.pallas import tpu as pltpu
from jax.sharding import PartitionSpec as P

SWEEPS = 3
SOURCE = 16.0
CENTRE = 1.075
HALFWIDTH = 0.925

OBS_AXES = ("z", "xh")
CELL_AXES = ("y", "xl", "core")
PLANE = ("xh", "y", "xl")
LAYERS = 16
GROUP = 16
ROWS = 256
TESTS = 64
NY, NZ = 8, 128
F32, BF16 = jnp.float32, jnp.bfloat16

VMEM = pl.BlockSpec(memory_space=pltpu.VMEM)
SMEM = pl.BlockSpec(memory_space=pltpu.SMEM)


def call(kernel, outs, specs, scratch=(), flops=0, moved=0):
    return pl.pallas_call(
        kernel,
        out_shape=outs,
        in_specs=specs,
        out_specs=jax.tree.map(lambda _: VMEM, outs),
        scratch_shapes=list(scratch),
        compiler_params=pltpu.CompilerParams(vmem_limit_bytes=40 * 2**20),
        cost_estimate=pl.CostEstimate(flops=flops, bytes_accessed=moved, transcendentals=0),
    )


def shape(*dims, dtype=F32):
    return jax.ShapeDtypeStruct(dims, dtype)


def places():
    row = lax.broadcasted_iota(jnp.int32, (NY, NZ), 0)
    col = lax.broadcasted_iota(jnp.int32, (NY, NZ), 1)
    return row, col


def beside(v):
    return (
        pltpu.roll(v, 1, 0),
        pltpu.roll(v, NY - 1, 0),
        pltpu.roll(v, 1, 1),
        pltpu.roll(v, NZ - 1, 1),
    )


def inside():
    row, col = places()
    return (row > 0, row < NY - 1, col > 0, col < NZ - 1)


def pack_kernel(logk_ref, label_ref, start_ref, packed_ref, conduct_ref):
    label = label_ref[0]
    logk = jnp.zeros((NY, NZ), F32)
    for zone in range(logk_ref.shape[0]):
        logk = jnp.where(label == zone, logk_ref[zone], logk)
    conduct = jnp.exp(logk)
    conduct_ref[...] = conduct
    for target in range(LAYERS):
        packed_ref[target, 0:GROUP] = start_ref[target]
        packed_ref[target, GROUP] = conduct


def sweep_kernel(me_ref, cell_ref, got_ref, out_ref, weight_ref, source_ref):
    row, col = places()
    flat = row * NZ + col
    inner = inside()

    def face(a, b):
        return 2.0 * a * b / (a + b)

    below = None
    for layer in range(LAYERS):
        here = got_ref[layer, GROUP]
        above = face(here, got_ref[layer + 1, GROUP]) if layer + 1 < LAYERS else None
        edge = [face(here, b) for b in beside(here)]
        faces = [here if below is None else below, here if above is None else above]
        faces += [jnp.where(ok, w, here) for ok, w in zip(inner, edge)]
        diagonal = faces[0]
        for extra in faces[1:]:
            diagonal = diagonal + extra
        inverse = 1.0 / diagonal
        if below is not None:
            weight_ref[layer, 0] = below * inverse
        if above is not None:
            weight_ref[layer, 1] = above * inverse
        for i, (ok, w) in enumerate(zip(inner, edge)):
            weight_ref[layer, 2 + i] = jnp.where(ok, w, 0.0) * inverse
        weight_ref[layer, 6] = inverse
        source_ref[layer] = jnp.zeros((NY, NZ), F32)
        below = above

    ratio = CENTRE / HALFWIDTH
    first = me_ref[0] * GROUP

    def one(k, carry):
        cell = cell_ref[first + k]
        layer_of = cell // (NY * NZ)
        hit = flat == cell - layer_of * (NY * NZ)
        source_ref[layer_of] = jnp.where(hit, SOURCE * weight_ref[layer_of, 6], 0.0)
        v = [got_ref[layer, k] for layer in range(LAYERS)]
        update = None
        damping = 1.0 / ratio
        for sweep in range(SWEEPS):
            misfit = []
            for layer in range(LAYERS):
                m = source_ref[layer] - v[layer]
                if layer > 0:
                    m = m + weight_ref[layer, 0] * v[layer - 1]
                if layer + 1 < LAYERS:
                    m = m + weight_ref[layer, 1] * v[layer + 1]
                for i, b in enumerate(beside(v[layer])):
                    m = m + weight_ref[layer, 2 + i] * b
                misfit.append(m)
            if sweep == 0:
                update = [m * (1.0 / CENTRE) for m in misfit]
            else:
                newer = 1.0 / (2.0 * ratio - damping)
                keep, add = newer * damping, 2.0 * newer / HALFWIDTH
                update = [keep * u + add * m for u, m in zip(update, misfit)]
                damping = newer
            v = [a + u for a, u in zip(v, update)]
        for layer in range(LAYERS):
            out_ref[layer, k, 0] = v[layer]
            if layer == 0:
                slope = v[1]
            elif layer + 1 == LAYERS:
                slope = -v[layer - 1]
            else:
                slope = v[layer + 1] - v[layer - 1]
            out_ref[layer, k, 1] = slope * 0.5
        source_ref[layer_of] = jnp.zeros((NY, NZ), F32)
        return carry

    lax.fori_loop(0, GROUP, one, 0)


def sensitivity_kernel(
    me_ref, test_ref, conduct_ref, heads_ref, low_ref, high_ref, field_ref,
    sens_ref, keep_ref, send_ref, slope_ref,
):
    ok = [jnp.where(o, 0.5, 0.0).astype(F32) for o in inside()]

    def along_y(v):
        return ok[1] * pltpu.roll(v, NY - 1, 0) - ok[0] * pltpu.roll(v, 1, 0)

    def along_z(v):
        return ok[3] * pltpu.roll(v, NZ - 1, 1) - ok[2] * pltpu.roll(v, 1, 1)

    factor = -conduct_ref[...]

    def slopes(t, carry):
        h = heads_ref[t]
        slope_ref[t, 0] = factor * ((high_ref[t] - low_ref[t]) * 0.5)
        slope_ref[t, 1] = factor * along_y(h)
        slope_ref[t, 2] = factor * along_z(h)
        return carry

    lax.fori_loop(0, TESTS, slopes, 0, unroll=4)
    mine = me_ref[1]

    def eight(block, carry):
        for i in range(8):
            k = block * 8 + i
            t = test_ref[k]
            v = field_ref[k, 0]
            total = field_ref[k, 1] * slope_ref[t, 0]
            total = total + along_y(v) * slope_ref[t, 1]
            total = total + along_z(v) * slope_ref[t, 2]
            sens_ref[pl.ds(pl.multiple_of(k * NY, NY), NY), :] = total
        here = pl.ds(pl.multiple_of(block * 8, 8), 8)
        for i in range(NY // 2):
            at = block * 64 + i
            lanes = pl.ds(i * NZ, NZ)
            keep_ref[here, lanes] = sens_ref[pl.ds(at + mine * (NY // 2), 8, stride=NY), :]
            send_ref[here, lanes] = sens_ref[pl.ds(at + (1 - mine) * (NY // 2), 8, stride=NY), :]
        return carry

    lax.fori_loop(0, ROWS // 8, eight, 0)


def split_into(ref, high_ref, low_ref, at, which):
    x = ref[...]
    high = x.astype(BF16)
    high_ref[at, which] = high
    low_ref[at, which] = (x - high.astype(F32)).astype(BF16)


def product(high_ref, low_ref, left, right):
    def dot(a, b):
        return lax.dot_general(a, b, (((1,), (1,)), ((), ())), preferred_element_type=F32)

    lh, ll = high_ref[left], low_ref[left]
    rh, rl = high_ref[right], low_ref[right]
    return dot(lh, rh) + (dot(lh, rl) + dot(ll, rh))


def near_kernel(me_ref, a0, b0, a1, b1, am, bm, mine_ref, theirs_ref, high_ref, low_ref):
    for at, pair in enumerate(((a0, b0), (a1, b1), (am, bm))):
        for which, ref in enumerate(pair):
            split_into(ref, high_ref, low_ref, at, which)
    xh, core = me_ref[1], me_ref[2]
    for side, out_ref in enumerate((mine_ref, theirs_ref)):
        right = side ^ core ^ xh
        for d, (a, b) in enumerate(((0, 0), (0, 1), (2, 1))):
            for half in range(2):
                block = product(high_ref, low_ref, (a, half ^ xh), (b, right))
                out_ref[:, 2 * d + half] = block.reshape(16, 16, ROWS)


def far_kernel(me_ref, am, bm, a2, b2, an, bn, mine_ref, theirs_ref, high_ref, low_ref):
    for at, pair in enumerate(((am, bm), (a2, b2), (an, bn))):
        for which, ref in enumerate(pair):
            split_into(ref, high_ref, low_ref, at, which)
    xh, core, late = me_ref[1], me_ref[2], me_ref[4]
    for side, out_ref in enumerate((mine_ref, theirs_ref)):
        right = side ^ core ^ xh
        for half in range(2):
            block = product(high_ref, low_ref, (0, half ^ xh), (1, right))
            out_ref[:, half] = block.reshape(16, 16, ROWS)
        block = product(high_ref, low_ref, (1 + late, late ^ xh), (2 - late, right))
        out_ref[:, 2] = block.reshape(16, 16, ROWS)


def total_kernel(parts_ref, out_ref):
    total = parts_ref[0]
    for i in range(1, parts_ref.shape[0]):
        total = total + parts_ref[i]
    out_ref[...] = total


def opposite(me_ref, up2, down2):
    first = me_ref[5] == 1
    return jnp.where(first, up2[2], down2[0]), jnp.where(first, down2[0], up2[2])


def give_kernel(me_ref, up1, up2, down2, give_ref):
    other = 1 - me_ref[2]
    give_ref[0] = up1[other]
    give_ref[1] = up1[2 + other]
    give_ref[2] = up2[other]
    pair = opposite(me_ref, up2, down2)
    give_ref[3] = jnp.where(other == 0, pair[0], pair[1])


def place_kernel(me_ref, near, up1, down1, up2, down2, got, slot_ref):
    core, z, first = me_ref[2], me_ref[3], me_ref[5]
    for r in range(4):
        for half in range(2):
            source = near[2 * r + half] if r < 2 else down1[2 * (r - 2) + half]
            slot_ref[half, (z + r) % 8] = source
    for i, (r, ref, at) in enumerate(((7, up1, 0), (6, up1, 2), (5, up2, 0))):
        slot_ref[core, (z + r) % 8] = ref[at + core]
        slot_ref[1 - core, (z + r) % 8] = got[i]
    pair = opposite(me_ref, up2, down2)
    own = jnp.where(core == 0, pair[0], pair[1])
    mine = jnp.where(first == 1, jnp.where(core == 0, pair[0], pair[1]), own)
    others = jnp.where(first == 1, jnp.where(core == 0, pair[1], pair[0]), got[3])
    slot_ref[core, (z + 4) % 8] = mine
    slot_ref[1 - core, (z + 4) % 8] = others


def finish_kernel(me_ref, block_ref, out_ref):
    flip = me_ref[6] == 1
    scale = 1.0 / (LAYERS * NY * NZ)

    @pl.when(flip)
    def _():
        out_ref[...] = block_ref[...].T * scale

    @pl.when(jnp.logical_not(flip))
    def _():
        out_ref[...] = block_ref[...] * scale


def swap(x, axis):
    return lax.ppermute(x, axis, [(0, 1), (1, 0)])


def round_z(x, by):
    return lax.ppermute(x, "z", [(i, (i + by) % 8) for i in range(8)])


def per_device(adjoint_start, forward_heads, zone_label, zone_logk, obs_cell, test_of_obs):
    cells = lax.axis_index(CELL_AXES)
    xh, core, z = lax.axis_index("xh"), lax.axis_index("core"), lax.axis_index("z")
    z2 = lax.axis_index(("y", "xl"))
    late = (z >= 4).astype(jnp.int32)
    first = ((z >= 2) & (z < 6)).astype(jnp.int32)
    r = (z2 - z + 8) % 8
    flip = ((r >= 5) | ((r == 4) & (first == 0))).astype(jnp.int32)
    me = jnp.stack([cells, xh, core, z, late, first, flip, flip]).astype(jnp.int32)

    heads = forward_heads.reshape(TESTS, NY, NZ)
    low = lax.ppermute(heads, CELL_AXES, [(i, i + 1) for i in range(LAYERS - 1)])
    high = lax.ppermute(heads, CELL_AXES, [(i + 1, i) for i in range(LAYERS - 1)])

    packed, conduct = call(
        pack_kernel,
        (shape(LAYERS, GROUP + 1, NY, NZ), shape(NY, NZ)),
        [SMEM, VMEM, VMEM],
    )(zone_logk, zone_label, adjoint_start.reshape(LAYERS, GROUP, NY, NZ))
    got = lax.all_to_all(packed, CELL_AXES, 0, 0, tiled=True)
    swept = call(
        sweep_kernel,
        shape(LAYERS, GROUP, 2, NY, NZ),
        [SMEM, SMEM, VMEM],
        [pltpu.VMEM((LAYERS, 7, NY, NZ), F32), pltpu.VMEM((LAYERS, NY, NZ), F32)],
    )(me, obs_cell, got)
    field = lax.all_to_all(swept, CELL_AXES, 0, 0, tiled=True).reshape(ROWS, 2, NY, NZ)

    half = NY * NZ // 2
    sens, a0, send = call(
        sensitivity_kernel,
        (shape(ROWS * NY, NZ), shape(ROWS, half), shape(ROWS, half)),
        [SMEM, SMEM, VMEM, VMEM, VMEM, VMEM, VMEM],
        [pltpu.VMEM((TESTS, 3, NY, NZ), F32)],
    )(me, test_of_obs, conduct, heads, low, high, field)

    a1, am = round_z(a0, -1), round_z(a0, 1)
    b0 = swap(send, "xh")
    b1, bm = round_z(b0, -1), round_z(b0, 1)
    a2, an = round_z(a1, -1), round_z(am, 1)
    b2, bn = round_z(b1, -1), round_z(bm, 1)

    def partial(kernel, count, *blocks):
        scratch = [pltpu.VMEM((3, 2, ROWS, half), BF16)] * 2
        out = shape(16, count, 16, ROWS)
        mine, theirs = call(
            kernel, (out, out), [SMEM] + [VMEM] * 6, scratch,
            flops=2 * 6 * count * ROWS * ROWS * half, moved=2**23,
        )(me, *blocks)
        both = mine + swap(theirs, "core")
        parts = lax.all_to_all(both, PLANE, 0, 0, tiled=True)
        return call(total_kernel, shape(count, 16, ROWS), [VMEM])(parts)

    near = partial(near_kernel, 6, a0, b0, a1, b1, am, bm)
    far = partial(far_kernel, 3, am, bm, a2, b2, an, bn)

    up1 = round_z(near[2:6], 1)
    down1 = round_z(jnp.concatenate([near[4:6], far[0:2]]), -1)
    up2 = round_z(far, 2)
    down2 = round_z(far[2:3], -2)
    give = call(give_kernel, shape(4, 16, ROWS), [SMEM] + [VMEM] * 3)(me, up1, up2, down2)
    swapped = swap(give, "core")
    slots = call(place_kernel, shape(2, 8, 16, ROWS), [SMEM] + [VMEM] * 6)(
        me, near, up1, down1, up2, down2, swapped
    )
    block = lax.all_to_all(slots.reshape(16, 16, ROWS), PLANE, 0, 0, tiled=True)
    gram = call(finish_kernel, shape(ROWS, ROWS), [SMEM, VMEM])(me, block.reshape(ROWS, ROWS))
    return sens.reshape(ROWS, 1, NY, NZ), gram


def solution(mesh):
    fine = jax.sharding.Mesh(
        mesh.devices.reshape(8, 2, 4, 2, 2), ("z", "xh", "y", "xl", "core")
    )
    return jax.shard_map(
        per_device,
        mesh=fine,
        in_specs=(
            P(OBS_AXES, CELL_AXES, None, None),
            P(None, CELL_AXES, None, None),
            P(CELL_AXES, None, None),
            P(),
            P(OBS_AXES),
            P(OBS_AXES),
        ),
        out_specs=(P(OBS_AXES, CELL_AXES, None, None), P(OBS_AXES, CELL_AXES)),
        check_vma=False,
    )
```

```python
import functools

import jax
import jax.numpy as jnp
from jax import lax
from jax.experimental import pallas as pl
from jax.experimental.pallas import tpu as pltpu
from jax.sharding import PartitionSpec as P

SWEEPS = 3
SOURCE = 16.0
CENTRE = 1.075
HALFWIDTH = 0.925

OBS_AXES = ("z", "xh")
CELL_AXES = ("y", "xl", "core")
PLANE = ("xh", "y", "xl")
LAYERS = 16
GROUP = 16
ROWS = 256
TESTS = 64
NY, NZ = 8, 128
F32, BF16 = jnp.float32, jnp.bfloat16

VMEM = pl.BlockSpec(memory_space=pltpu.VMEM)
SMEM = pl.BlockSpec(memory_space=pltpu.SMEM)
HBM = pl.BlockSpec(memory_space=pltpu.HBM)


def call(kernel, outs, specs, scratch=(), flops=0, moved=0):
    return pl.pallas_call(
        kernel,
        out_shape=outs,
        in_specs=specs,
        out_specs=jax.tree.map(lambda _: VMEM, outs),
        scratch_shapes=list(scratch),
        compiler_params=pltpu.CompilerParams(vmem_limit_bytes=40 * 2**20),
        cost_estimate=pl.CostEstimate(flops=flops, bytes_accessed=moved, transcendentals=0),
    )


def shape(*dims, dtype=F32):
    return jax.ShapeDtypeStruct(dims, dtype)


def places():
    row = lax.broadcasted_iota(jnp.int32, (NY, NZ), 0)
    col = lax.broadcasted_iota(jnp.int32, (NY, NZ), 1)
    return row, col


def beside(v):
    return (
        pltpu.roll(v, 1, 0),
        pltpu.roll(v, NY - 1, 0),
        pltpu.roll(v, 1, 1),
        pltpu.roll(v, NZ - 1, 1),
    )


def inside():
    row, col = places()
    return (row > 0, row < NY - 1, col > 0, col < NZ - 1)


def pack_kernel(
    logk_hbm, test_hbm, label_hbm, start_hbm, heads_hbm, packed_hbm,
    logk_ref, test_ref, label_ref, heads_ref, packed_ref, sems,
):
    moves = [
        pltpu.make_async_copy(source, target, sems.at[i])
        for i, (source, target) in enumerate((
            (heads_hbm, heads_ref),
            (test_hbm, test_ref),
            (logk_hbm, logk_ref),
            (label_hbm, label_ref),
            (start_hbm, packed_ref.at[:, pl.ds(0, GROUP)]),
        ))
    ]
    for move in moves:
        move.start()
    moves[2].wait()
    moves[3].wait()
    label = label_ref[0]
    logk = jnp.zeros((NY, NZ), F32)
    for zone in range(logk_ref.shape[0]):
        logk = jnp.where(label == zone, logk_ref[zone], logk)
    conduct = jnp.exp(logk)
    moves[0].wait()
    moves[1].wait()

    def one(target, carry):
        for k in range(GROUP):
            packed_ref[target, GROUP + k] = heads_ref[test_ref[target * GROUP + k]]
        packed_ref[target, 2 * GROUP] = conduct
        return carry

    lax.fori_loop(0, LAYERS, one, 0)
    moves[4].wait()
    out = pltpu.make_async_copy(packed_ref, packed_hbm, sems.at[5])
    out.start()
    out.wait()


def sweep_kernel(me_ref, cell_ref, got_ref, panel_ref, out_ref, weight_ref, source_ref):
    row, col = places()
    flat = row * NZ + col
    inner = inside()
    mask = [jnp.where(ok, 1.0, 0.0).astype(F32) for ok in inner]

    def along_x(v, layer):
        if layer == 0:
            return v[1]
        if layer + 1 == LAYERS:
            return -v[layer - 1]
        return v[layer + 1] - v[layer - 1]

    def along_y(v):
        return mask[1] * pltpu.roll(v, NY - 1, 0) - mask[0] * pltpu.roll(v, 1, 0)

    def along_z(v):
        return mask[3] * pltpu.roll(v, NZ - 1, 1) - mask[2] * pltpu.roll(v, 1, 1)

    def face(a, b):
        return 2.0 * a * b / (a + b)

    below = None
    for layer in range(LAYERS):
        here = got_ref[layer, 2 * GROUP]
        above = face(here, got_ref[layer + 1, 2 * GROUP]) if layer + 1 < LAYERS else None
        edge = [face(here, b) for b in beside(here)]
        faces = [here if below is None else below, here if above is None else above]
        faces += [jnp.where(ok, w, here) for ok, w in zip(inner, edge)]
        diagonal = faces[0]
        for extra in faces[1:]:
            diagonal = diagonal + extra
        inverse = 1.0 / diagonal
        if below is not None:
            weight_ref[layer, 0] = below * inverse
        if above is not None:
            weight_ref[layer, 1] = above * inverse
        for i, (ok, w) in enumerate(zip(inner, edge)):
            weight_ref[layer, 2 + i] = jnp.where(ok, w, 0.0) * inverse
        weight_ref[layer, 6] = inverse
        source_ref[layer] = jnp.zeros((NY, NZ), F32)
        below = above

    ratio = CENTRE / HALFWIDTH
    first = me_ref[0] * GROUP

    def one(k, carry):
        cell = cell_ref[first + k]
        layer_of = cell // (NY * NZ)
        hit = flat == cell - layer_of * (NY * NZ)
        source_ref[layer_of] = jnp.where(hit, SOURCE * weight_ref[layer_of, 6], 0.0)
        v = [got_ref[layer, k] for layer in range(LAYERS)]
        update = None
        damping = 1.0 / ratio
        for sweep in range(SWEEPS):
            misfit = []
            for layer in range(LAYERS):
                m = source_ref[layer] - v[layer]
                if layer > 0:
                    m = m + weight_ref[layer, 0] * v[layer - 1]
                if layer + 1 < LAYERS:
                    m = m + weight_ref[layer, 1] * v[layer + 1]
                for i, b in enumerate(beside(v[layer])):
                    m = m + weight_ref[layer, 2 + i] * b
                misfit.append(m)
            if sweep == 0:
                update = [m * (1.0 / CENTRE) for m in misfit]
            else:
                newer = 1.0 / (2.0 * ratio - damping)
                keep, add = newer * damping, 2.0 * newer / HALFWIDTH
                update = [keep * u + add * m for u, m in zip(update, misfit)]
                damping = newer
            v = [a + u for a, u in zip(v, update)]
        h = [got_ref[layer, GROUP + k] for layer in range(LAYERS)]
        for layer in range(LAYERS):
            total = along_x(v, layer) * along_x(h, layer)
            total = total + along_y(v[layer]) * along_y(h[layer])
            total = total + along_z(v[layer]) * along_z(h[layer])
            here = pl.ds(pl.multiple_of(k * NY, NY), NY)
            out_ref[layer, here, :] = (-0.25 * got_ref[layer, 2 * GROUP]) * total
        source_ref[layer_of] = jnp.zeros((NY, NZ), F32)
        return carry

    lax.fori_loop(0, GROUP, one, 0)

    def panel(layer, carry):
        for part in range(2):
            for i in range(NY // 2):
                at = part * (NY // 2) + i
                rows = out_ref[layer, pl.ds(at, GROUP, stride=NY), :]
                panel_ref[part * LAYERS + layer, :, pl.ds(i * NZ, NZ)] = rows
        return carry

    lax.fori_loop(0, LAYERS, panel, 0)


def split_into(ref, high_ref, low_ref, at):
    x = ref[...]
    high = x.astype(BF16)
    high_ref[at] = high
    low_ref[at] = (x - high.astype(F32)).astype(BF16)


def product(high_ref, low_ref, left, right):
    def dot(a, b):
        return lax.dot_general(a, b, (((1,), (1,)), ((), ())), preferred_element_type=F32)

    lh, ll = high_ref[left], low_ref[left]
    rh, rl = high_ref[right], low_ref[right]
    return dot(lh, rh) + (dot(lh, rl) + dot(ll, rh))


def rows_of(which):
    return pl.ds(pl.multiple_of(which * ROWS, ROWS), ROWS)


def pair_kernel(pairs, me_ref, *refs):
    blocks, (mine_ref, theirs_ref, high_ref, low_ref) = refs[:-4], refs[-4:]
    for at, ref in enumerate(blocks):
        split_into(ref, high_ref, low_ref, at)
    core = me_ref[2]
    for side, out_ref in enumerate((mine_ref, theirs_ref)):
        right = rows_of(side ^ core)
        for i, (a, b) in enumerate(pairs):
            for half in range(2):
                block = product(high_ref, low_ref, (a, rows_of(half)), (b, right))
                out_ref[half, :, i] = block.reshape(8, 32, ROWS)


def sens_kernel(me_ref, panel_ref, got_ref, sens_ref):
    xh = me_ref[1]

    def eight(block, carry):
        own = pl.ds(pl.multiple_of(xh * ROWS + block * 8, 8), 8)
        here = pl.ds(pl.multiple_of(block * 8, 8), 8)
        at = block * (8 * NY)
        for i in range(NY // 2):
            lanes = pl.ds(i * NZ, NZ)
            sens_ref[pl.ds(at + xh * (NY // 2) + i, 8, stride=NY), :] = panel_ref[own, lanes]
            sens_ref[pl.ds(at + (1 - xh) * (NY // 2) + i, 8, stride=NY), :] = got_ref[here, lanes]
        return carry

    lax.fori_loop(0, ROWS // 8, eight, 0, unroll=4)


def total_kernel(parts_ref, out_ref):
    total = parts_ref[0]
    for i in range(1, parts_ref.shape[0]):
        total = total + parts_ref[i]
    out_ref[...] = total


def place_kernel(me_ref, d0, d12, up1, down1, far_down1, up2, down2, slot_ref):
    z = me_ref[3]
    sources = (d0[0], d12[0], down1[0], far_down1[0], down2[0], up2[0], up1[1], up1[0])
    for r, source in enumerate(sources):
        slot_ref[(z + r) % 8] = source


def finish_kernel(me_ref, block_ref, out_ref):
    flip = me_ref[4] == 1
    scale = 1.0 / (LAYERS * NY * NZ)

    @pl.when(flip)
    def _():
        out_ref[...] = block_ref[...].T * scale

    @pl.when(jnp.logical_not(flip))
    def _():
        out_ref[...] = block_ref[...] * scale


def swap(x, axis):
    return lax.ppermute(x, axis, [(0, 1), (1, 0)])


def round_z(x, by):
    return lax.ppermute(x, "z", [(i, (i + by) % 8) for i in range(8)])


def turn_z(x, by):
    pairs = [
        ((z * 2 + a) * 2 + b, (((z + by) % 8) * 2 + b) * 2 + a)
        for z in range(8) for a in range(2) for b in range(2)
    ]
    return lax.ppermute(x, ("z", "xh", "core"), pairs)


def per_device(adjoint_start, forward_heads, zone_label, zone_logk, obs_cell, test_of_obs):
    cells = lax.axis_index(CELL_AXES)
    xh, core, z = lax.axis_index("xh"), lax.axis_index("core"), lax.axis_index("z")
    z2 = lax.axis_index(("y", "xl"))
    flip = ((z2 - z + 8) % 8 >= 5).astype(jnp.int32)
    me = jnp.stack([cells, xh, core, z, flip, flip, flip, flip]).astype(jnp.int32)

    packed = pl.pallas_call(
        pack_kernel,
        out_shape=shape(LAYERS, 2 * GROUP + 1, NY, NZ),
        in_specs=[HBM] * 5,
        out_specs=HBM,
        scratch_shapes=[
            pltpu.SMEM((zone_logk.shape[0],), F32),
            pltpu.SMEM((ROWS,), jnp.int32),
            pltpu.VMEM((1, NY, NZ), jnp.int32),
            pltpu.VMEM((TESTS, NY, NZ), F32),
            pltpu.VMEM((LAYERS, 2 * GROUP + 1, NY, NZ), F32),
            pltpu.SemaphoreType.DMA((6,)),
        ],
        compiler_params=pltpu.CompilerParams(vmem_limit_bytes=60 * 2**20),
    )(
        zone_logk, test_of_obs, zone_label,
        adjoint_start.reshape(LAYERS, GROUP, NY, NZ), forward_heads.reshape(TESTS, NY, NZ),
    )
    got = lax.all_to_all(packed, CELL_AXES, 0, 0, tiled=True)
    half = NY * NZ // 2
    panel = call(
        sweep_kernel,
        shape(2 * LAYERS, GROUP, half),
        [SMEM, SMEM, VMEM],
        [
            pltpu.VMEM((LAYERS, GROUP * NY, NZ), F32),
            pltpu.VMEM((LAYERS, 7, NY, NZ), F32),
            pltpu.VMEM((LAYERS, NY, NZ), F32),
        ],
    )(me, obs_cell, got)
    x0 = lax.all_to_all(panel, ("xh",) + CELL_AXES, 0, 0, tiled=True).reshape(2 * ROWS, half)
    x1, xm = round_z(x0, -1), round_z(x0, 1)
    other = swap(lax.dynamic_slice(x0, ((1 - xh) * ROWS, 0), (ROWS, half)), "xh")
    x2, xn = round_z(x1, -1), round_z(xm, 1)

    def partial(pairs, *blocks):
        count = len(pairs)
        out = shape(2, 8, count, 32, ROWS)
        mine, theirs = call(
            functools.partial(pair_kernel, pairs),
            (out, out),
            [SMEM] + [VMEM] * len(blocks),
            [pltpu.VMEM((len(blocks), 2 * ROWS, half), BF16)] * 2,
            flops=24 * count * ROWS * ROWS * half, moved=2**23,
        )(me, *blocks)
        return mine + swap(theirs, "core")

    def exchange(parts):
        parts = parts.reshape(16, parts.shape[2], 32, ROWS)
        return lax.all_to_all(parts, PLANE, 0, 0, tiled=True)

    def total(parts):
        return call(total_kernel, shape(*parts.shape[1:]), [VMEM])(parts)

    d0 = exchange(partial(((0, 0),), x0))
    x1, xm, d0, other = lax.optimization_barrier((x1, xm, d0, other))
    d12 = partial(((0, 1), (2, 1)), x0, x1, xm)
    d12, other = lax.optimization_barrier((d12, other))
    sens = call(sens_kernel, shape(ROWS * NY, NZ), [SMEM, VMEM, VMEM])(me, x0, other)
    d12 = exchange(d12)
    d12, x2, xn, sens = lax.optimization_barrier((d12, x2, xn, sens))
    far = total(exchange(partial(((0, 1), (2, 1)), xm, x2, xn)))
    d0, d12 = total(d0), total(d12)

    slots = call(place_kernel, shape(8, 32, ROWS), [SMEM] + [VMEM] * 7)(
        me, d0, d12,
        turn_z(d12, 1), round_z(d12[1:2], -1),
        round_z(far[0:1], -1), turn_z(far[0:1], 2), round_z(far[1:2], -2),
    )
    block = lax.all_to_all(slots, ("y", "xl"), 0, 0, tiled=True)
    gram = call(finish_kernel, shape(ROWS, ROWS), [SMEM, VMEM])(me, block.reshape(ROWS, ROWS))
    return sens.reshape(ROWS, 1, NY, NZ), gram


def solution(mesh):
    fine = jax.sharding.Mesh(
        mesh.devices.reshape(8, 2, 4, 2, 2), ("z", "xh", "y", "xl", "core")
    )
    return jax.shard_map(
        per_device,
        mesh=fine,
        in_specs=(
            P(OBS_AXES, CELL_AXES, None, None),
            P(None, CELL_AXES, None, None),
            P(CELL_AXES, None, None),
            P(),
            P(OBS_AXES),
            P(OBS_AXES),
        ),
        out_specs=(P(OBS_AXES, CELL_AXES, None, None), P(OBS_AXES, CELL_AXES)),
        check_vma=False,
    )
```

```python
import functools

import jax
import jax.numpy as jnp
from jax import lax
from jax.experimental import pallas as pl
from jax.experimental.pallas import tpu as pltpu
from jax.sharding import PartitionSpec as P

SWEEPS = 3
SOURCE = 16.0
CENTRE = 1.075
HALFWIDTH = 0.925

OBS_AXES = ("z", "xh")
CELL_AXES = ("y", "xl", "core")
PLANE = ("xh", "y", "xl")
LAYERS = 16
GROUP = 16
ROWS = 256
TESTS = 64
NY, NZ = 8, 128
F32, BF16 = jnp.float32, jnp.bfloat16

VMEM = pl.BlockSpec(memory_space=pltpu.VMEM)
SMEM = pl.BlockSpec(memory_space=pltpu.SMEM)
HBM = pl.BlockSpec(memory_space=pltpu.HBM)


def call(kernel, outs, specs, scratch=(), flops=0, moved=0):
    return pl.pallas_call(
        kernel,
        out_shape=outs,
        in_specs=specs,
        out_specs=jax.tree.map(lambda _: VMEM, outs),
        scratch_shapes=list(scratch),
        compiler_params=pltpu.CompilerParams(vmem_limit_bytes=40 * 2**20),
        cost_estimate=pl.CostEstimate(flops=flops, bytes_accessed=moved, transcendentals=0),
    )


def shape(*dims, dtype=F32):
    return jax.ShapeDtypeStruct(dims, dtype)


def places():
    row = lax.broadcasted_iota(jnp.int32, (NY, NZ), 0)
    col = lax.broadcasted_iota(jnp.int32, (NY, NZ), 1)
    return row, col


def beside(v):
    return (
        pltpu.roll(v, 1, 0),
        pltpu.roll(v, NY - 1, 0),
        pltpu.roll(v, 1, 1),
        pltpu.roll(v, NZ - 1, 1),
    )


def inside():
    row, col = places()
    return (row > 0, row < NY - 1, col > 0, col < NZ - 1)


def pack_kernel(
    logk_hbm, test_hbm, label_hbm, start_hbm, heads_hbm, packed_hbm,
    logk_ref, test_ref, label_ref, heads_ref, packed_ref, sems,
):
    moves = [
        pltpu.make_async_copy(source, target, sems.at[i])
        for i, (source, target) in enumerate((
            (heads_hbm, heads_ref),
            (test_hbm, test_ref),
            (logk_hbm, logk_ref),
            (label_hbm, label_ref),
            (start_hbm, packed_ref.at[:, pl.ds(0, GROUP)]),
        ))
    ]
    for move in moves:
        move.start()
    moves[2].wait()
    moves[3].wait()
    label = label_ref[0]
    logk = jnp.zeros((NY, NZ), F32)
    for zone in range(logk_ref.shape[0]):
        logk = jnp.where(label == zone, logk_ref[zone], logk)
    conduct = jnp.exp(logk)
    moves[0].wait()
    moves[1].wait()

    def one(target, carry):
        for k in range(GROUP):
            packed_ref[target, GROUP + k] = heads_ref[test_ref[target * GROUP + k]]
        packed_ref[target, 2 * GROUP] = conduct
        return carry

    lax.fori_loop(0, LAYERS, one, 0)
    moves[4].wait()
    out = pltpu.make_async_copy(packed_ref, packed_hbm, sems.at[5])
    out.start()
    out.wait()


def sweep_kernel(me_ref, cell_ref, got_ref, panel_ref, out_ref, weight_ref, source_ref):
    row, col = places()
    flat = row * NZ + col
    inner = inside()
    mask = [jnp.where(ok, 1.0, 0.0).astype(F32) for ok in inner]

    def along_x(v, layer):
        if layer == 0:
            return v[1]
        if layer + 1 == LAYERS:
            return -v[layer - 1]
        return v[layer + 1] - v[layer - 1]

    def along_y(v):
        return mask[1] * pltpu.roll(v, NY - 1, 0) - mask[0] * pltpu.roll(v, 1, 0)

    def along_z(v):
        return mask[3] * pltpu.roll(v, NZ - 1, 1) - mask[2] * pltpu.roll(v, 1, 1)

    def face(a, b):
        return 2.0 * a * b / (a + b)

    below = None
    for layer in range(LAYERS):
        here = got_ref[layer, 2 * GROUP]
        above = face(here, got_ref[layer + 1, 2 * GROUP]) if layer + 1 < LAYERS else None
        edge = [face(here, b) for b in beside(here)]
        faces = [here if below is None else below, here if above is None else above]
        faces += [jnp.where(ok, w, here) for ok, w in zip(inner, edge)]
        diagonal = faces[0]
        for extra in faces[1:]:
            diagonal = diagonal + extra
        inverse = 1.0 / diagonal
        if below is not None:
            weight_ref[layer, 0] = below * inverse
        if above is not None:
            weight_ref[layer, 1] = above * inverse
        for i, (ok, w) in enumerate(zip(inner, edge)):
            weight_ref[layer, 2 + i] = jnp.where(ok, w, 0.0) * inverse
        weight_ref[layer, 6] = inverse
        source_ref[layer] = jnp.zeros((NY, NZ), F32)
        below = above

    ratio = CENTRE / HALFWIDTH
    first = me_ref[0] * GROUP

    def one(k, carry):
        cell = cell_ref[first + k]
        layer_of = cell // (NY * NZ)
        hit = flat == cell - layer_of * (NY * NZ)
        source_ref[layer_of] = jnp.where(hit, SOURCE * weight_ref[layer_of, 6], 0.0)
        v = [got_ref[layer, k] for layer in range(LAYERS)]
        update = [None] * LAYERS
        damping = 1.0 / ratio
        for sweep in range(SWEEPS):
            newer = None if sweep == 0 else 1.0 / (2.0 * ratio - damping)
            fresh = []
            for layer in range(LAYERS):
                m = source_ref[layer] - v[layer]
                if layer > 0:
                    m = m + weight_ref[layer, 0] * v[layer - 1]
                if layer + 1 < LAYERS:
                    m = m + weight_ref[layer, 1] * v[layer + 1]
                for i, b in enumerate(beside(v[layer])):
                    m = m + weight_ref[layer, 2 + i] * b
                if sweep == 0:
                    update[layer] = m * (1.0 / CENTRE)
                else:
                    update[layer] = newer * damping * update[layer] + 2.0 * newer / HALFWIDTH * m
                fresh.append(v[layer] + update[layer])
            damping = damping if sweep == 0 else newer
            v = fresh
        h = [got_ref[layer, GROUP + k] for layer in range(LAYERS)]
        for layer in range(LAYERS):
            total = along_x(v, layer) * along_x(h, layer)
            total = total + along_y(v[layer]) * along_y(h[layer])
            total = total + along_z(v[layer]) * along_z(h[layer])
            here = pl.ds(pl.multiple_of(k * NY, NY), NY)
            out_ref[layer, here, :] = (-0.25 * got_ref[layer, 2 * GROUP]) * total
        source_ref[layer_of] = jnp.zeros((NY, NZ), F32)
        return carry

    lax.fori_loop(0, GROUP, one, 0, unroll=4)

    def panel(layer, carry):
        for part in range(2):
            for i in range(NY // 2):
                at = part * (NY // 2) + i
                rows = out_ref[layer, pl.ds(at, GROUP, stride=NY), :]
                panel_ref[part * LAYERS + layer, :, pl.ds(i * NZ, NZ)] = rows
        return carry

    lax.fori_loop(0, LAYERS, panel, 0)


def split_into(ref, high_ref, low_ref, at):
    x = ref[...]
    high = x.astype(BF16)
    high_ref[at] = high
    low_ref[at] = (x - high.astype(F32)).astype(BF16)


def product(high_ref, low_ref, left, right):
    def dot(a, b):
        return lax.dot_general(a, b, (((1,), (1,)), ((), ())), preferred_element_type=F32)

    lh, ll = high_ref[left], low_ref[left]
    rh, rl = high_ref[right], low_ref[right]
    return dot(lh, rh) + (dot(lh, rl) + dot(ll, rh))


def rows_of(which):
    return pl.ds(pl.multiple_of(which * ROWS, ROWS), ROWS)


def pair_kernel(pairs, side, me_ref, *refs):
    blocks, (out_ref, high_ref, low_ref) = refs[:-3], refs[-3:]
    for at, ref in enumerate(blocks):
        split_into(ref, high_ref, low_ref, at)
    right = rows_of(side ^ me_ref[2])
    for i, (a, b) in enumerate(pairs):
        block = product(high_ref, low_ref, a, (b, right))
        out_ref[:, :, i] = block.reshape(2, 8, 32, ROWS)


def sens_kernel(me_ref, panel_ref, got_ref, sens_ref):
    xh = me_ref[1]

    def eight(block, carry):
        own = pl.ds(pl.multiple_of(xh * ROWS + block * 8, 8), 8)
        here = pl.ds(pl.multiple_of(block * 8, 8), 8)
        at = block * (8 * NY)
        for i in range(NY // 2):
            lanes = pl.ds(i * NZ, NZ)
            sens_ref[pl.ds(at + xh * (NY // 2) + i, 8, stride=NY), :] = panel_ref[own, lanes]
            sens_ref[pl.ds(at + (1 - xh) * (NY // 2) + i, 8, stride=NY), :] = got_ref[here, lanes]
        return carry

    lax.fori_loop(0, ROWS // 8, eight, 0, unroll=4)


def total_kernel(parts_ref, out_ref):
    total = parts_ref[0]
    for i in range(1, parts_ref.shape[0]):
        total = total + parts_ref[i]
    out_ref[...] = total


def place_kernel(me_ref, d0, d12, up1, down1, down2, far_up1, slot_ref):
    z = me_ref[3]
    sources = (d0[0], d12[0], down1[0], down2[0], down2[1], far_up1[0], up1[1], up1[0])
    for r, source in enumerate(sources):
        slot_ref[(z + r) % 8] = source


def finish_kernel(me_ref, block_ref, out_ref):
    flip = me_ref[4] == 1
    scale = 1.0 / (LAYERS * NY * NZ)

    @pl.when(flip)
    def _():
        out_ref[...] = block_ref[...].T * scale

    @pl.when(jnp.logical_not(flip))
    def _():
        out_ref[...] = block_ref[...] * scale


def swap(x, axis):
    return lax.ppermute(x, axis, [(0, 1), (1, 0)])


def round_z(x, by):
    return lax.ppermute(x, "z", [(i, (i + by) % 8) for i in range(8)])


def turn_z(x, by):
    pairs = [
        ((z * 2 + a) * 2 + b, (((z + by) % 8) * 2 + b) * 2 + a)
        for z in range(8) for a in range(2) for b in range(2)
    ]
    return lax.ppermute(x, ("z", "xh", "core"), pairs)


def per_device(adjoint_start, forward_heads, zone_label, zone_logk, obs_cell, test_of_obs):
    cells = lax.axis_index(CELL_AXES)
    xh, core, z = lax.axis_index("xh"), lax.axis_index("core"), lax.axis_index("z")
    z2 = lax.axis_index(("y", "xl"))
    flip = ((z2 - z + 8) % 8 >= 5).astype(jnp.int32)
    me = jnp.stack([cells, xh, core, z, flip, flip, flip, flip]).astype(jnp.int32)

    packed = pl.pallas_call(
        pack_kernel,
        out_shape=shape(LAYERS, 2 * GROUP + 1, NY, NZ),
        in_specs=[HBM] * 5,
        out_specs=HBM,
        scratch_shapes=[
            pltpu.SMEM((zone_logk.shape[0],), F32),
            pltpu.SMEM((ROWS,), jnp.int32),
            pltpu.VMEM((1, NY, NZ), jnp.int32),
            pltpu.VMEM((TESTS, NY, NZ), F32),
            pltpu.VMEM((LAYERS, 2 * GROUP + 1, NY, NZ), F32),
            pltpu.SemaphoreType.DMA((6,)),
        ],
        compiler_params=pltpu.CompilerParams(vmem_limit_bytes=60 * 2**20),
    )(
        zone_logk, test_of_obs, zone_label,
        adjoint_start.reshape(LAYERS, GROUP, NY, NZ), forward_heads.reshape(TESTS, NY, NZ),
    )
    got = lax.all_to_all(packed, CELL_AXES, 0, 0, tiled=True)
    half = NY * NZ // 2
    panel = call(
        sweep_kernel,
        shape(2 * LAYERS, GROUP, half),
        [SMEM, SMEM, VMEM],
        [
            pltpu.VMEM((LAYERS, GROUP * NY, NZ), F32),
            pltpu.VMEM((LAYERS, 7, NY, NZ), F32),
            pltpu.VMEM((LAYERS, NY, NZ), F32),
        ],
    )(me, obs_cell, got)
    x0 = lax.all_to_all(panel, ("xh",) + CELL_AXES, 0, 0, tiled=True).reshape(2 * ROWS, half)
    x1, xm = round_z(x0, -1), round_z(x0, 1)
    x2, xn = round_z(x1, -1), round_z(xm, 1)

    def partial(pairs, *blocks):
        count = len(pairs)

        def share(side):
            return call(
                functools.partial(pair_kernel, pairs, side),
                shape(2, 8, count, 32, ROWS),
                [SMEM] + [VMEM] * len(blocks),
                [pltpu.VMEM((len(blocks), 2 * ROWS, half), BF16)] * 2,
                flops=12 * count * ROWS * ROWS * half, moved=2**22,
            )(me, *blocks)

        theirs = swap(share(1), "core")
        return share(0) + theirs

    def exchange(parts):
        parts = parts.reshape(16, parts.shape[2], 32, ROWS)
        return lax.all_to_all(parts, PLANE, 0, 0, tiled=True)

    def total(parts):
        return call(total_kernel, shape(*parts.shape[1:]), [VMEM])(parts)

    d0 = exchange(partial(((0, 0),), x0))
    other = swap(lax.dynamic_slice(x0, ((1 - xh) * ROWS, 0), (ROWS, half)), "xh")
    x1, xm, d0, other = lax.optimization_barrier((x1, xm, d0, other))
    d12 = partial(((0, 1), (2, 1)), x0, x1, xm)
    d12, other = lax.optimization_barrier((d12, other))
    sens = call(sens_kernel, shape(ROWS * NY, NZ), [SMEM, VMEM, VMEM])(me, x0, other)
    d12 = exchange(d12)
    d12, x2, xn, sens = lax.optimization_barrier((d12, x2, xn, sens))
    d0, d12 = total(d0), total(d12)
    up1, down1 = turn_z(d12, 1), round_z(d12[1:2], -1)
    far = exchange(partial(((0, 1), (0, 2)), xn, x1, x2))
    far, up1, down1 = lax.optimization_barrier((far, up1, down1))
    far = total(far)

    slots = call(place_kernel, shape(8, 32, ROWS), [SMEM] + [VMEM] * 6)(
        me, d0, d12, up1, down1, round_z(far, -2), turn_z(far[0:1], 1)
    )
    block = lax.all_to_all(slots, ("y", "xl"), 0, 0, tiled=True)
    gram = call(finish_kernel, shape(ROWS, ROWS), [SMEM, VMEM])(me, block.reshape(ROWS, ROWS))
    return sens.reshape(ROWS, 1, NY, NZ), gram


def solution(mesh):
    fine = jax.sharding.Mesh(
        mesh.devices.reshape(8, 2, 4, 2, 2), ("z", "xh", "y", "xl", "core")
    )
    return jax.shard_map(
        per_device,
        mesh=fine,
        in_specs=(
            P(OBS_AXES, CELL_AXES, None, None),
            P(None, CELL_AXES, None, None),
            P(CELL_AXES, None, None),
            P(),
            P(OBS_AXES),
            P(OBS_AXES),
        ),
        out_specs=(P(OBS_AXES, CELL_AXES, None, None), P(OBS_AXES, CELL_AXES)),
        check_vma=False,
    )
```

```python
import functools

import jax
import jax.numpy as jnp
from jax import lax
from jax.experimental import pallas as pl
from jax.experimental.pallas import tpu as pltpu
from jax.sharding import PartitionSpec as P

SWEEPS = 3
SOURCE = 16.0
CENTRE = 1.075
HALFWIDTH = 0.925

OBS_AXES = ("z", "xh")
CELL_AXES = ("y", "xl", "core")
PLANE = ("xh", "y", "xl")
LAYERS = 16
GROUP = 16
ROWS = 256
TESTS = 64
NY, NZ = 8, 128
F32, BF16 = jnp.float32, jnp.bfloat16

VMEM = pl.BlockSpec(memory_space=pltpu.VMEM)
SMEM = pl.BlockSpec(memory_space=pltpu.SMEM)
HBM = pl.BlockSpec(memory_space=pltpu.HBM)


def call(kernel, outs, specs, scratch=(), flops=0, moved=0):
    return pl.pallas_call(
        kernel,
        out_shape=outs,
        in_specs=specs,
        out_specs=jax.tree.map(lambda _: VMEM, outs),
        scratch_shapes=list(scratch),
        compiler_params=pltpu.CompilerParams(vmem_limit_bytes=40 * 2**20),
        cost_estimate=pl.CostEstimate(flops=flops, bytes_accessed=moved, transcendentals=0),
    )


def shape(*dims, dtype=F32):
    return jax.ShapeDtypeStruct(dims, dtype)


def places():
    row = lax.broadcasted_iota(jnp.int32, (NY, NZ), 0)
    col = lax.broadcasted_iota(jnp.int32, (NY, NZ), 1)
    return row, col


def beside(v):
    return (
        pltpu.roll(v, 1, 0),
        pltpu.roll(v, NY - 1, 0),
        pltpu.roll(v, 1, 1),
        pltpu.roll(v, NZ - 1, 1),
    )


def inside():
    row, col = places()
    return (row > 0, row < NY - 1, col > 0, col < NZ - 1)


def pack_kernel(
    logk_hbm, test_hbm, label_hbm, start_hbm, heads_hbm, packed_hbm,
    logk_ref, test_ref, label_ref, heads_ref, start_ref, rest_ref, sems,
):
    moves = [
        pltpu.make_async_copy(source, target, sems.at[i])
        for i, (source, target) in enumerate((
            (heads_hbm, heads_ref),
            (test_hbm, test_ref),
            (logk_hbm, logk_ref),
            (label_hbm, label_ref),
            (start_hbm, start_ref),
        ))
    ]
    for move in moves:
        move.start()
    moves[2].wait()
    moves[3].wait()
    label = label_ref[0]
    logk = jnp.zeros((NY, NZ), F32)
    for zone in range(logk_ref.shape[0]):
        logk = jnp.where(label == zone, logk_ref[zone], logk)
    conduct = jnp.exp(logk)
    moves[0].wait()
    moves[1].wait()
    moves[4].wait()
    early = pltpu.make_async_copy(start_ref, packed_hbm.at[:, pl.ds(0, GROUP)], sems.at[5])
    early.start()

    def one(target, carry):
        for k in range(GROUP):
            rest_ref[target, k] = heads_ref[test_ref[target * GROUP + k]]
        rest_ref[target, GROUP] = conduct
        return carry

    lax.fori_loop(0, LAYERS, one, 0)
    late = pltpu.make_async_copy(rest_ref, packed_hbm.at[:, pl.ds(GROUP, GROUP + 1)], sems.at[6])
    late.start()
    early.wait()
    late.wait()


def sweep_kernel(me_ref, cell_ref, got_ref, panel_ref, out_ref, weight_ref, source_ref):
    row, col = places()
    flat = row * NZ + col
    inner = inside()
    mask = [jnp.where(ok, 1.0, 0.0).astype(F32) for ok in inner]

    def along_x(v, layer):
        if layer == 0:
            return v[1]
        if layer + 1 == LAYERS:
            return -v[layer - 1]
        return v[layer + 1] - v[layer - 1]

    def along_y(v):
        return mask[1] * pltpu.roll(v, NY - 1, 0) - mask[0] * pltpu.roll(v, 1, 0)

    def along_z(v):
        return mask[3] * pltpu.roll(v, NZ - 1, 1) - mask[2] * pltpu.roll(v, 1, 1)

    def face(a, b):
        return 2.0 * a * b / (a + b)

    below = None
    for layer in range(LAYERS):
        here = got_ref[layer, 2 * GROUP]
        above = face(here, got_ref[layer + 1, 2 * GROUP]) if layer + 1 < LAYERS else None
        edge = [face(here, b) for b in beside(here)]
        faces = [here if below is None else below, here if above is None else above]
        faces += [jnp.where(ok, w, here) for ok, w in zip(inner, edge)]
        diagonal = faces[0]
        for extra in faces[1:]:
            diagonal = diagonal + extra
        inverse = 1.0 / diagonal
        if below is not None:
            weight_ref[layer, 0] = below * inverse
        if above is not None:
            weight_ref[layer, 1] = above * inverse
        for i, (ok, w) in enumerate(zip(inner, edge)):
            weight_ref[layer, 2 + i] = jnp.where(ok, w, 0.0) * inverse
        weight_ref[layer, 6] = inverse
        source_ref[layer] = jnp.zeros((NY, NZ), F32)
        below = above

    ratio = CENTRE / HALFWIDTH
    first = me_ref[0] * GROUP

    def one(k, carry):
        cell = cell_ref[first + k]
        layer_of = cell // (NY * NZ)
        hit = flat == cell - layer_of * (NY * NZ)
        source_ref[layer_of] = jnp.where(hit, SOURCE * weight_ref[layer_of, 6], 0.0)
        v = [got_ref[layer, k] for layer in range(LAYERS)]
        update = [None] * LAYERS
        damping = 1.0 / ratio
        for sweep in range(SWEEPS):
            newer = None if sweep == 0 else 1.0 / (2.0 * ratio - damping)
            fresh = []
            for layer in range(LAYERS):
                m = source_ref[layer] - v[layer]
                if layer > 0:
                    m = m + weight_ref[layer, 0] * v[layer - 1]
                if layer + 1 < LAYERS:
                    m = m + weight_ref[layer, 1] * v[layer + 1]
                for i, b in enumerate(beside(v[layer])):
                    m = m + weight_ref[layer, 2 + i] * b
                if sweep == 0:
                    update[layer] = m * (1.0 / CENTRE)
                else:
                    update[layer] = newer * damping * update[layer] + 2.0 * newer / HALFWIDTH * m
                fresh.append(v[layer] + update[layer])
            damping = damping if sweep == 0 else newer
            v = fresh
        h = [got_ref[layer, GROUP + k] for layer in range(LAYERS)]
        for layer in range(LAYERS):
            total = along_x(v, layer) * along_x(h, layer)
            total = total + along_y(v[layer]) * along_y(h[layer])
            total = total + along_z(v[layer]) * along_z(h[layer])
            here = pl.ds(pl.multiple_of(k * NY, NY), NY)
            out_ref[layer, here, :] = (-0.25 * got_ref[layer, 2 * GROUP]) * total
        source_ref[layer_of] = jnp.zeros((NY, NZ), F32)
        return carry

    lax.fori_loop(0, GROUP, one, 0, unroll=4)

    def panel(layer, carry):
        for part in range(2):
            for i in range(NY // 2):
                at = part * (NY // 2) + i
                rows = out_ref[layer, pl.ds(at, GROUP, stride=NY), :]
                panel_ref[part * LAYERS + layer, :, pl.ds(i * NZ, NZ)] = rows
        return carry

    lax.fori_loop(0, LAYERS, panel, 0)


def split_into(ref, high_ref, low_ref, at):
    x = ref[...]
    high = x.astype(BF16)
    high_ref[at] = high
    low_ref[at] = (x - high.astype(F32)).astype(BF16)


def product(high_ref, low_ref, left, right):
    def dot(a, b):
        return lax.dot_general(a, b, (((1,), (1,)), ((), ())), preferred_element_type=F32)

    lh, ll = high_ref[left], low_ref[left]
    rh, rl = high_ref[right], low_ref[right]
    return dot(lh, rh) + (dot(lh, rl) + dot(ll, rh))


def rows_of(which):
    return pl.ds(pl.multiple_of(which * ROWS, ROWS), ROWS)


def pair_kernel(pairs, side, me_ref, *refs):
    blocks, (out_ref, high_ref, low_ref) = refs[:-3], refs[-3:]
    for at, ref in enumerate(blocks):
        split_into(ref, high_ref, low_ref, at)
    right = rows_of(side ^ me_ref[2])
    for i, (a, b) in enumerate(pairs):
        block = product(high_ref, low_ref, a, (b, right))
        out_ref[:, :, i] = block.reshape(2, 8, 32, ROWS)


def sens_kernel(me_ref, panel_ref, got_ref, sens_ref):
    xh = me_ref[1]

    def eight(block, carry):
        own = pl.ds(pl.multiple_of(xh * ROWS + block * 8, 8), 8)
        here = pl.ds(pl.multiple_of(block * 8, 8), 8)
        at = block * (8 * NY)
        for i in range(NY // 2):
            lanes = pl.ds(i * NZ, NZ)
            sens_ref[pl.ds(at + xh * (NY // 2) + i, 8, stride=NY), :] = panel_ref[own, lanes]
            sens_ref[pl.ds(at + (1 - xh) * (NY // 2) + i, 8, stride=NY), :] = got_ref[here, lanes]
        return carry

    lax.fori_loop(0, ROWS // 8, eight, 0, unroll=4)


def total_kernel(parts_ref, out_ref):
    total = parts_ref[0]
    for i in range(1, parts_ref.shape[0]):
        total = total + parts_ref[i]
    out_ref[...] = total


def place_kernel(me_ref, d0, d12, up1, down1, down2, far_up1, slot_ref):
    z = me_ref[3]
    sources = (d0[0], d12[0], down1[0], down2[0], down2[1], far_up1[0], up1[1], up1[0])
    for r, source in enumerate(sources):
        slot_ref[(z + r) % 8] = source


def finish_kernel(me_ref, block_ref, out_ref):
    flip = me_ref[4] == 1
    scale = 1.0 / (LAYERS * NY * NZ)

    @pl.when(flip)
    def _():
        out_ref[...] = block_ref[...].T * scale

    @pl.when(jnp.logical_not(flip))
    def _():
        out_ref[...] = block_ref[...] * scale


def swap(x, axis):
    return lax.ppermute(x, axis, [(0, 1), (1, 0)])


def round_z(x, by):
    return lax.ppermute(x, "z", [(i, (i + by) % 8) for i in range(8)])


def turn_z(x, by):
    pairs = [
        ((z * 2 + a) * 2 + b, (((z + by) % 8) * 2 + b) * 2 + a)
        for z in range(8) for a in range(2) for b in range(2)
    ]
    return lax.ppermute(x, ("z", "xh", "core"), pairs)


def per_device(adjoint_start, forward_heads, zone_label, zone_logk, obs_cell, test_of_obs):
    cells = lax.axis_index(CELL_AXES)
    xh, core, z = lax.axis_index("xh"), lax.axis_index("core"), lax.axis_index("z")
    z2 = lax.axis_index(("y", "xl"))
    flip = ((z2 - z + 8) % 8 >= 5).astype(jnp.int32)
    me = jnp.stack([cells, xh, core, z, flip, flip, flip, flip]).astype(jnp.int32)

    packed = pl.pallas_call(
        pack_kernel,
        out_shape=shape(LAYERS, 2 * GROUP + 1, NY, NZ),
        in_specs=[HBM] * 5,
        out_specs=HBM,
        scratch_shapes=[
            pltpu.SMEM((zone_logk.shape[0],), F32),
            pltpu.SMEM((ROWS,), jnp.int32),
            pltpu.VMEM((1, NY, NZ), jnp.int32),
            pltpu.VMEM((TESTS, NY, NZ), F32),
            pltpu.VMEM((LAYERS, GROUP, NY, NZ), F32),
            pltpu.VMEM((LAYERS, GROUP + 1, NY, NZ), F32),
            pltpu.SemaphoreType.DMA((7,)),
        ],
        compiler_params=pltpu.CompilerParams(vmem_limit_bytes=60 * 2**20),
    )(
        zone_logk, test_of_obs, zone_label,
        adjoint_start.reshape(LAYERS, GROUP, NY, NZ), forward_heads.reshape(TESTS, NY, NZ),
    )
    got = lax.all_to_all(packed, CELL_AXES, 0, 0, tiled=True)
    half = NY * NZ // 2
    panel = call(
        sweep_kernel,
        shape(2 * LAYERS, GROUP, half),
        [SMEM, SMEM, VMEM],
        [
            pltpu.VMEM((LAYERS, GROUP * NY, NZ), F32),
            pltpu.VMEM((LAYERS, 7, NY, NZ), F32),
            pltpu.VMEM((LAYERS, NY, NZ), F32),
        ],
    )(me, obs_cell, got)
    x0 = lax.all_to_all(panel, ("xh",) + CELL_AXES, 0, 0, tiled=True).reshape(2 * ROWS, half)
    x1, xm = round_z(x0, -1), round_z(x0, 1)
    x2, xn = round_z(x1, -1), round_z(xm, 1)

    def partial(pairs, *blocks):
        count = len(pairs)

        def share(side):
            return call(
                functools.partial(pair_kernel, pairs, side),
                shape(2, 8, count, 32, ROWS),
                [SMEM] + [VMEM] * len(blocks),
                [pltpu.VMEM((len(blocks), 2 * ROWS, half), BF16)] * 2,
                flops=12 * count * ROWS * ROWS * half, moved=2**22,
            )(me, *blocks)

        theirs = swap(share(1), "core")
        return share(0) + theirs

    def exchange(parts):
        parts = parts.reshape(16, parts.shape[2], 32, ROWS)
        return lax.all_to_all(parts, PLANE, 0, 0, tiled=True)

    def total(parts):
        return call(total_kernel, shape(*parts.shape[1:]), [VMEM])(parts)

    d0 = exchange(partial(((0, 0),), x0))
    other = swap(lax.dynamic_slice(x0, ((1 - xh) * ROWS, 0), (ROWS, half)), "xh")
    x1, xm, d0, other = lax.optimization_barrier((x1, xm, d0, other))
    d12 = partial(((0, 1), (2, 1)), x0, x1, xm)
    d12, other = lax.optimization_barrier((d12, other))
    sens = call(sens_kernel, shape(ROWS * NY, NZ), [SMEM, VMEM, VMEM])(me, x0, other)
    d12 = exchange(d12)
    d12, x2, xn, sens = lax.optimization_barrier((d12, x2, xn, sens))
    d0, d12 = total(d0), total(d12)
    up1, down1 = turn_z(d12, 1), round_z(d12[1:2], -1)
    far = exchange(partial(((0, 1), (0, 2)), xn, x1, x2))
    far, up1, down1 = lax.optimization_barrier((far, up1, down1))
    far = total(far)

    slots = call(place_kernel, shape(8, 32, ROWS), [SMEM] + [VMEM] * 6)(
        me, d0, d12, up1, down1, round_z(far, -2), turn_z(far[0:1], 1)
    )
    block = lax.all_to_all(slots, ("y", "xl"), 0, 0, tiled=True)
    gram = call(finish_kernel, shape(ROWS, ROWS), [SMEM, VMEM])(me, block.reshape(ROWS, ROWS))
    return sens.reshape(ROWS, 1, NY, NZ), gram


def solution(mesh):
    fine = jax.sharding.Mesh(
        mesh.devices.reshape(8, 2, 4, 2, 2), ("z", "xh", "y", "xl", "core")
    )
    return jax.shard_map(
        per_device,
        mesh=fine,
        in_specs=(
            P(OBS_AXES, CELL_AXES, None, None),
            P(None, CELL_AXES, None, None),
            P(CELL_AXES, None, None),
            P(),
            P(OBS_AXES),
            P(OBS_AXES),
        ),
        out_specs=(P(OBS_AXES, CELL_AXES, None, None), P(OBS_AXES, CELL_AXES)),
        check_vma=False,
    )
```

```python
import functools

import jax
import jax.numpy as jnp
from jax import lax
from jax.experimental import pallas as pl
from jax.experimental.pallas import tpu as pltpu
from jax.sharding import PartitionSpec as P

SWEEPS = 3
SOURCE = 16.0
CENTRE = 1.075
HALFWIDTH = 0.925

OBS_AXES = ("z", "xh")
CELL_AXES = ("y", "xl", "core")
PLANE = ("xh", "y", "xl")
LAYERS = 16
GROUP = 16
ROWS = 256
TESTS = 64
NY, NZ = 8, 128
F32, BF16 = jnp.float32, jnp.bfloat16

VMEM = pl.BlockSpec(memory_space=pltpu.VMEM)
SMEM = pl.BlockSpec(memory_space=pltpu.SMEM)
HBM = pl.BlockSpec(memory_space=pltpu.HBM)


def call(kernel, outs, specs, scratch=(), flops=0, moved=0):
    return pl.pallas_call(
        kernel,
        out_shape=outs,
        in_specs=specs,
        out_specs=jax.tree.map(lambda _: VMEM, outs),
        scratch_shapes=list(scratch),
        compiler_params=pltpu.CompilerParams(vmem_limit_bytes=40 * 2**20),
        cost_estimate=pl.CostEstimate(flops=flops, bytes_accessed=moved, transcendentals=0),
    )


def shape(*dims, dtype=F32):
    return jax.ShapeDtypeStruct(dims, dtype)


def places():
    row = lax.broadcasted_iota(jnp.int32, (NY, NZ), 0)
    col = lax.broadcasted_iota(jnp.int32, (NY, NZ), 1)
    return row, col


def beside(v):
    return (
        pltpu.roll(v, 1, 0),
        pltpu.roll(v, NY - 1, 0),
        pltpu.roll(v, 1, 1),
        pltpu.roll(v, NZ - 1, 1),
    )


def inside():
    row, col = places()
    return (row > 0, row < NY - 1, col > 0, col < NZ - 1)


def pack_kernel(
    logk_hbm, test_hbm, label_hbm, start_hbm, heads_hbm, packed_hbm,
    logk_ref, test_ref, label_ref, heads_ref, packed_ref, sems,
):
    moves = [
        pltpu.make_async_copy(source, target, sems.at[i])
        for i, (source, target) in enumerate((
            (heads_hbm, heads_ref),
            (test_hbm, test_ref),
            (logk_hbm, logk_ref),
            (label_hbm, label_ref),
            (start_hbm, packed_ref.at[:, pl.ds(0, GROUP)]),
        ))
    ]
    for move in moves:
        move.start()
    moves[2].wait()
    moves[3].wait()
    label = label_ref[0]
    logk = jnp.zeros((NY, NZ), F32)
    for zone in range(logk_ref.shape[0]):
        logk = jnp.where(label == zone, logk_ref[zone], logk)
    conduct = jnp.exp(logk)
    moves[0].wait()
    moves[1].wait()

    def one(target, carry):
        for k in range(GROUP):
            packed_ref[target, GROUP + k] = heads_ref[test_ref[target * GROUP + k]]
        packed_ref[target, 2 * GROUP] = conduct
        return carry

    lax.fori_loop(0, LAYERS, one, 0)
    moves[4].wait()
    out = pltpu.make_async_copy(packed_ref, packed_hbm, sems.at[5])
    out.start()
    out.wait()


def sweep_kernel(me_ref, cell_ref, got_ref, panel_ref, out_ref, weight_ref, source_ref):
    row, col = places()
    flat = row * NZ + col
    inner = inside()
    mask = [jnp.where(ok, 1.0, 0.0).astype(F32) for ok in inner]

    def along_x(v, layer):
        if layer == 0:
            return v[1]
        if layer + 1 == LAYERS:
            return -v[layer - 1]
        return v[layer + 1] - v[layer - 1]

    def along_y(v):
        return mask[1] * pltpu.roll(v, NY - 1, 0) - mask[0] * pltpu.roll(v, 1, 0)

    def along_z(v):
        return mask[3] * pltpu.roll(v, NZ - 1, 1) - mask[2] * pltpu.roll(v, 1, 1)

    def face(a, b):
        return 2.0 * a * b / (a + b)

    below = None
    for layer in range(LAYERS):
        here = got_ref[layer, 2 * GROUP]
        above = face(here, got_ref[layer + 1, 2 * GROUP]) if layer + 1 < LAYERS else None
        edge = [face(here, b) for b in beside(here)]
        faces = [here if below is None else below, here if above is None else above]
        faces += [jnp.where(ok, w, here) for ok, w in zip(inner, edge)]
        diagonal = faces[0]
        for extra in faces[1:]:
            diagonal = diagonal + extra
        inverse = 1.0 / diagonal
        if below is not None:
            weight_ref[layer, 0] = below * inverse
        if above is not None:
            weight_ref[layer, 1] = above * inverse
        for i, (ok, w) in enumerate(zip(inner, edge)):
            weight_ref[layer, 2 + i] = jnp.where(ok, w, 0.0) * inverse
        weight_ref[layer, 6] = inverse
        source_ref[layer] = jnp.zeros((NY, NZ), F32)
        below = above

    ratio = CENTRE / HALFWIDTH
    first = me_ref[0] * GROUP

    def one(k, carry):
        cell = cell_ref[first + k]
        layer_of = cell // (NY * NZ)
        hit = flat == cell - layer_of * (NY * NZ)
        source_ref[layer_of] = jnp.where(hit, SOURCE * weight_ref[layer_of, 6], 0.0)
        v = [got_ref[layer, k] for layer in range(LAYERS)]
        update = [None] * LAYERS
        damping = 1.0 / ratio
        for sweep in range(SWEEPS):
            newer = None if sweep == 0 else 1.0 / (2.0 * ratio - damping)
            fresh = []
            for layer in range(LAYERS):
                m = source_ref[layer] - v[layer]
                if layer > 0:
                    m = m + weight_ref[layer, 0] * v[layer - 1]
                if layer + 1 < LAYERS:
                    m = m + weight_ref[layer, 1] * v[layer + 1]
                for i, b in enumerate(beside(v[layer])):
                    m = m + weight_ref[layer, 2 + i] * b
                if sweep == 0:
                    update[layer] = m * (1.0 / CENTRE)
                else:
                    update[layer] = newer * damping * update[layer] + 2.0 * newer / HALFWIDTH * m
                fresh.append(v[layer] + update[layer])
            damping = damping if sweep == 0 else newer
            v = fresh
        h = [got_ref[layer, GROUP + k] for layer in range(LAYERS)]
        for layer in range(LAYERS):
            total = along_x(v, layer) * along_x(h, layer)
            total = total + along_y(v[layer]) * along_y(h[layer])
            total = total + along_z(v[layer]) * along_z(h[layer])
            here = pl.ds(pl.multiple_of(k * NY, NY), NY)
            out_ref[layer, here, :] = (-0.25 * got_ref[layer, 2 * GROUP]) * total
        source_ref[layer_of] = jnp.zeros((NY, NZ), F32)
        return carry

    lax.fori_loop(0, GROUP, one, 0, unroll=4)

    def panel(layer, carry):
        for part in range(2):
            for i in range(NY // 2):
                at = part * (NY // 2) + i
                rows = out_ref[layer, pl.ds(at, GROUP, stride=NY), :]
                panel_ref[part * LAYERS + layer, :, pl.ds(i * NZ, NZ)] = rows
        return carry

    lax.fori_loop(0, LAYERS, panel, 0)


def split_into(ref, high_ref, low_ref, at):
    x = ref[...]
    high = x.astype(BF16)
    high_ref[at] = high
    low_ref[at] = (x - high.astype(F32)).astype(BF16)


def product(high_ref, low_ref, left, right):
    def dot(a, b):
        return lax.dot_general(a, b, (((1,), (1,)), ((), ())), preferred_element_type=F32)

    lh, ll = high_ref[left], low_ref[left]
    rh, rl = high_ref[right], low_ref[right]
    return dot(lh, rh) + (dot(lh, rl) + dot(ll, rh))


def rows_of(which):
    return pl.ds(pl.multiple_of(which * ROWS, ROWS), ROWS)


def pair_kernel(pairs, side, me_ref, *refs):
    blocks, (out_ref, high_ref, low_ref) = refs[:-3], refs[-3:]
    for at, ref in enumerate(blocks):
        split_into(ref, high_ref, low_ref, at)
    right = rows_of(side ^ me_ref[2])
    for i, (a, b) in enumerate(pairs):
        block = product(high_ref, low_ref, a, (b, right))
        out_ref[:, :, i] = block.reshape(2, 8, 32, ROWS)


def sens_kernel(me_ref, panel_ref, got_ref, sens_ref):
    xh = me_ref[1]

    def eight(block, carry):
        own = pl.ds(pl.multiple_of(xh * ROWS + block * 8, 8), 8)
        here = pl.ds(pl.multiple_of(block * 8, 8), 8)
        at = block * (8 * NY)
        for i in range(NY // 2):
            lanes = pl.ds(i * NZ, NZ)
            sens_ref[pl.ds(at + xh * (NY // 2) + i, 8, stride=NY), :] = panel_ref[own, lanes]
            sens_ref[pl.ds(at + (1 - xh) * (NY // 2) + i, 8, stride=NY), :] = got_ref[here, lanes]
        return carry

    lax.fori_loop(0, ROWS // 8, eight, 0, unroll=4)


def total_kernel(parts_ref, out_ref):
    total = parts_ref[0]
    for i in range(1, parts_ref.shape[0]):
        total = total + parts_ref[i]
    out_ref[...] = total


def place_kernel(me_ref, d0, d12, up1, down1, down2, far_up1, slot_ref):
    z = me_ref[3]
    sources = (d0[0], d12[0], down1[0], down2[0], down2[1], far_up1[0], up1[1], up1[0])
    for r, source in enumerate(sources):
        slot_ref[(z + r) % 8] = source


def finish_kernel(me_ref, block_ref, out_ref):
    flip = me_ref[4] == 1
    scale = 1.0 / (LAYERS * NY * NZ)

    @pl.when(flip)
    def _():
        out_ref[...] = block_ref[...].T * scale

    @pl.when(jnp.logical_not(flip))
    def _():
        out_ref[...] = block_ref[...] * scale


def swap(x, axis):
    return lax.ppermute(x, axis, [(0, 1), (1, 0)])


def round_z(x, by):
    return lax.ppermute(x, "z", [(i, (i + by) % 8) for i in range(8)])


def turn_z(x, by):
    pairs = [
        ((z * 2 + a) * 2 + b, (((z + by) % 8) * 2 + b) * 2 + a)
        for z in range(8) for a in range(2) for b in range(2)
    ]
    return lax.ppermute(x, ("z", "xh", "core"), pairs)


def per_device(adjoint_start, forward_heads, zone_label, zone_logk, obs_cell, test_of_obs):
    cells = lax.axis_index(CELL_AXES)
    xh, core, z = lax.axis_index("xh"), lax.axis_index("core"), lax.axis_index("z")
    z2 = lax.axis_index(("y", "xl"))
    flip = ((z2 - z + 8) % 8 >= 5).astype(jnp.int32)
    me = jnp.stack([cells, xh, core, z, flip, flip, flip, flip]).astype(jnp.int32)

    packed = pl.pallas_call(
        pack_kernel,
        out_shape=shape(LAYERS, 2 * GROUP + 1, NY, NZ),
        in_specs=[HBM] * 5,
        out_specs=HBM,
        scratch_shapes=[
            pltpu.SMEM((zone_logk.shape[0],), F32),
            pltpu.SMEM((ROWS,), jnp.int32),
            pltpu.VMEM((1, NY, NZ), jnp.int32),
            pltpu.VMEM((TESTS, NY, NZ), F32),
            pltpu.VMEM((LAYERS, 2 * GROUP + 1, NY, NZ), F32),
            pltpu.SemaphoreType.DMA((6,)),
        ],
        compiler_params=pltpu.CompilerParams(vmem_limit_bytes=60 * 2**20),
    )(
        zone_logk, test_of_obs, zone_label,
        adjoint_start.reshape(LAYERS, GROUP, NY, NZ), forward_heads.reshape(TESTS, NY, NZ),
    )
    got = lax.all_to_all(packed, CELL_AXES, 0, 0, tiled=True)
    half = NY * NZ // 2
    panel = call(
        sweep_kernel,
        shape(2 * LAYERS, GROUP, half),
        [SMEM, SMEM, VMEM],
        [
            pltpu.VMEM((LAYERS, GROUP * NY, NZ), F32),
            pltpu.VMEM((LAYERS, 7, NY, NZ), F32),
            pltpu.VMEM((LAYERS, NY, NZ), F32),
        ],
    )(me, obs_cell, got)
    x0 = lax.all_to_all(panel, ("xh",) + CELL_AXES, 0, 0, tiled=True).reshape(2 * ROWS, half)
    x1, xm = round_z(x0, -1), round_z(x0, 1)
    x2, xn = round_z(x1, -1), round_z(xm, 1)

    def partial(pairs, *blocks):
        count = len(pairs)

        def share(side):
            return call(
                functools.partial(pair_kernel, pairs, side),
                shape(2, 8, count, 32, ROWS),
                [SMEM] + [VMEM] * len(blocks),
                [pltpu.VMEM((len(blocks), 2 * ROWS, half), BF16)] * 2,
                flops=12 * count * ROWS * ROWS * half, moved=2**22,
            )(me, *blocks)

        theirs = swap(share(1), "core")
        return share(0) + theirs

    def exchange(parts):
        parts = parts.reshape(16, parts.shape[2], 32, ROWS)
        return lax.all_to_all(parts, PLANE, 0, 0, tiled=True)

    def total(parts):
        return call(total_kernel, shape(*parts.shape[1:]), [VMEM])(parts)

    d0 = exchange(partial(((0, 0),), x0))
    other = lax.dynamic_slice(x0, ((1 - xh) * ROWS, 0), (ROWS, half))
    x1, xm, d0, other = lax.optimization_barrier((x1, xm, d0, other))
    d12 = exchange(partial(((0, 1), (2, 1)), x0, x1, xm))
    d12, x2, xn = lax.optimization_barrier((d12, x2, xn))
    d0, d12 = total(d0), total(d12)
    up1, down1 = turn_z(d12, 1), round_z(d12[1:2], -1)
    far = exchange(partial(((0, 1), (0, 2)), xn, x1, x2))
    far, up1, down1, other = lax.optimization_barrier((far, up1, down1, other))
    far = total(far)
    sens = call(sens_kernel, shape(ROWS * NY, NZ), [SMEM, VMEM, VMEM])(me, x0, swap(other, "xh"))

    slots = call(place_kernel, shape(8, 32, ROWS), [SMEM] + [VMEM] * 6)(
        me, d0, d12, up1, down1, round_z(far, -2), turn_z(far[0:1], 1)
    )
    block = lax.all_to_all(slots, ("y", "xl"), 0, 0, tiled=True)
    block, sens = lax.optimization_barrier((block, sens))
    gram = call(finish_kernel, shape(ROWS, ROWS), [SMEM, VMEM])(me, block.reshape(ROWS, ROWS))
    return sens.reshape(ROWS, 1, NY, NZ), gram


def solution(mesh):
    fine = jax.sharding.Mesh(
        mesh.devices.reshape(8, 2, 4, 2, 2), ("z", "xh", "y", "xl", "core")
    )
    return jax.shard_map(
        per_device,
        mesh=fine,
        in_specs=(
            P(OBS_AXES, CELL_AXES, None, None),
            P(None, CELL_AXES, None, None),
            P(CELL_AXES, None, None),
            P(),
            P(OBS_AXES),
            P(OBS_AXES),
        ),
        out_specs=(P(OBS_AXES, CELL_AXES, None, None), P(OBS_AXES, CELL_AXES)),
        check_vma=False,
    )
```
